256 devices in a mesh: tm: 8 (over x, y_hi), space: 32 (over y_lo, z, core).
Axes of the slice: x: 4, y: 4 (y_hi: 2, y_lo: 2; y = y_hi * 2 + y_lo), z: 8, core: 2. Of those that a mesh axis runs over, the one named last changes fastest.
Arguments:
- latents: bfloat16 [512, 16, 15360], P('tm', None, 'space'), may hold values from -6 to 6
- conv_kernel: bfloat16 [16, 144], replicated, may hold values from -0.5 to 0.5
- codebook: bfloat16 [16, 65536], replicated, may hold values from -6 to 6
- fine_codes: int32 [256, 15360], P('tm', 'space'), may hold values from 0 to 65535
- coarse_codes: int32 [256, 15360], P(('tm', 'space')), may hold values from 0 to 65535
Outputs:
- fine_error: bfloat16 [256, 16, 15360], P('tm', None, 'space')
- coarse_error: bfloat16 [256, 16, 15360], P(('tm', 'space'))
- code_sums: float32 [16, 65536], P(None, ('tm', 'space'))
The draws below stay inside these ranges and needn't reach their ends.
All inputs are finite; a program needn't handle non-finite values.
Results may differ from the reference program's by a relative error of at most 0.011.
Values may be sent and summed in bfloat16 or wider, within the bound.
No kernel may reach another device: no remote copies, remote signals or barrier semaphores. Data moves between devices by JAX's collectives and lax.ppermute only.
A program may use at most 256 MiB of HBM per device.

```python
import jax
import jax.numpy as jnp
from jax import lax

CHANNELS = 16
CODES = 65536
WIDTH = 240
FRAMES = 512
HEIGHT = 64
PIXELS = 15360


def place_ends(entries, rng, smallest, high):
    index_at = [jax.random.randint(jax.random.fold_in(rng, axis), (), 0, length) for axis, length in enumerate(entries.shape)]
    widest = entries.shape.index(max(entries.shape))
    next_to = index_at[:widest] + [(index_at[widest] + 1) % entries.shape[widest]] + index_at[widest + 1:]
    return entries.at[tuple(index_at)].set(smallest).at[tuple(next_to)].set(high)


def level_of(rng, shape, cuts, smallest, top_value):
    factor_of = 1.0
    for axis_at, shards_of in cuts:
        draws = jax.random.uniform(jax.random.fold_in(jax.random.fold_in(rng, 6), axis_at), (shards_of,), jnp.float32, smallest / len(cuts), top_value / len(cuts))
        factor_of = factor_of * jnp.repeat(jnp.exp(draws), shape[axis_at] // shards_of).reshape((-1,) + (1,) * (len(shape) - 1 - axis_at))
    return factor_of


def scatter_about(stream_key, extent, width, most, shards=(), kind=jnp.bfloat16):
    result = width * jax.random.normal(stream_key, extent, jnp.float32)
    if shards:
        result = result * level_of(stream_key, extent, shards, -0.22, 0.18)
    return jnp.clip(result, -most, most).astype(kind)


def setup_inputs(seed: int = 0) -> dict:
    keys = jax.random.split(jax.random.key(seed), 6)
    return {
        "latents": scatter_about(keys[0], (FRAMES, CHANNELS, PIXELS), 1.0, 6.0, ((0, 8), (2, 32))),
        "conv_kernel": scatter_about(keys[1], (CHANNELS, 9 * CHANNELS), (9 * CHANNELS) ** -0.5, 0.5),
        "codebook": scatter_about(keys[2], (CHANNELS, CODES), 1.0, 6.0),
        "fine_codes": place_ends(jax.random.randint(keys[3], (FRAMES // 2, PIXELS), 0, CODES), jax.random.fold_in(keys[3], 1), 0, CODES - 1).astype(jnp.int32),
        "coarse_codes": place_ends(jax.random.randint(keys[4], (FRAMES // 2, PIXELS), 0, CODES), jax.random.fold_in(keys[4], 1), 0, CODES - 1).astype(jnp.int32),
    }


def tap_stack(detail_frame):
    grid = detail_frame.reshape(CHANNELS, HEIGHT, WIDTH)
    padded = jnp.pad(grid, ((0, 0), (1, 1), (1, 1)))
    pieces = []
    for row_shift in range(3):
        for col_shift in range(3):
            pieces.append(padded[:, row_shift:row_shift + HEIGHT, col_shift:col_shift + WIDTH].reshape(CHANNELS, PIXELS))
    return jnp.concatenate(pieces, axis=0)


def lift_four(frame_a, frame_b, frame_c, frame_d, position_axis):
    detail_left = (frame_b.astype(jnp.float32) - frame_a.astype(jnp.float32)).astype(jnp.bfloat16)
    smooth_left = (frame_a.astype(jnp.float32) + 0.5 * detail_left.astype(jnp.float32)).astype(jnp.bfloat16)
    detail_right = (frame_d.astype(jnp.float32) - frame_c.astype(jnp.float32)).astype(jnp.bfloat16)
    smooth_right = (frame_c.astype(jnp.float32) + 0.5 * detail_right.astype(jnp.float32)).astype(jnp.bfloat16)
    detail_top = (smooth_right.astype(jnp.float32) - smooth_left.astype(jnp.float32)).astype(jnp.bfloat16)
    smooth_top = (smooth_left.astype(jnp.float32) + 0.5 * detail_top.astype(jnp.float32)).astype(jnp.bfloat16)
    return jnp.stack([smooth_top, detail_left, detail_top, detail_right], axis=position_axis)


def reference(latents, conv_kernel, codebook, fine_codes, coarse_codes):
    frame_pairs = latents.reshape(FRAMES // 2, 2, CHANNELS, PIXELS)

    def fine_step(running, inputs):
        pair_frames, code_ids = inputs
        even_frame = pair_frames[0].astype(jnp.float32)
        odd_frame = pair_frames[1].astype(jnp.float32)
        detail = (odd_frame - even_frame).astype(jnp.bfloat16)
        low_band = (even_frame + 0.5 * detail.astype(jnp.float32)).astype(jnp.bfloat16)
        encoded = detail.astype(jnp.float32) + jnp.dot(conv_kernel, tap_stack(detail), preferred_element_type=jnp.float32)
        looked = codebook[:, code_ids].astype(jnp.float32)
        quant_error = (encoded - looked).astype(jnp.bfloat16)
        running = running.at[:, code_ids].add(encoded)
        return running, (low_band, quant_error)

    running = jnp.zeros((CHANNELS, CODES), jnp.float32)
    running, (low_band, fine_error) = lax.scan(fine_step, running, (frame_pairs, fine_codes))
    groups = low_band.reshape(FRAMES // 8, 4, CHANNELS, PIXELS)
    lifted = lax.map(lambda group_frames: lift_four(group_frames[0], group_frames[1], group_frames[2], group_frames[3], 0), groups)
    coarse = lifted.reshape(FRAMES // 2, CHANNELS, PIXELS)

    def coarse_step(running, inputs):
        coarse_frame, code_ids = inputs
        values = coarse_frame.astype(jnp.float32)
        quant_error = (values - codebook[:, code_ids].astype(jnp.float32)).astype(jnp.bfloat16)
        running = running.at[:, code_ids].add(values)
        return running, quant_error

    running, coarse_error = lax.scan(coarse_step, running, (coarse, coarse_codes))
    return fine_error, coarse_error, running
```

```python
import jax
import jax.numpy as jnp
import numpy as np
from jax import lax
from jax.experimental import pallas as pl
from jax.experimental.pallas import tpu as pltpu
from jax.sharding import Mesh, PartitionSpec as P

CHANNELS = 16
CODES = 65536
WIDTH = 240
TILE = 480
LINES = 32
ROWS = CODES // 4
TABLES = 4
MIB = 2**20
f32, bf16 = jnp.float32, jnp.bfloat16

SPACE = ("yl", "z", "core")
FRAMES_BY = ("x", "yh")
Y = ("yh", "yl")
CORES = ("x", "yh", "yl", "z", "core")

VMEM = pl.BlockSpec(memory_space=pltpu.VMEM)
HBM = pl.BlockSpec(memory_space=pl.ANY)


def nt(a, b):
    return lax.dot_general(a, b, (((1,), (1,)), ((), ())), preferred_element_type=f32)


def tn(a, b):
    return lax.dot_general(a, b, (((0,), (0,)), ((), ())), preferred_element_type=f32)


def lift_kernel(lat_ref, detail_ref, head_ref, tail_ref, lifted_ref):
    def group(g, carry):
        low = []
        for k in range(4):
            even = lat_ref[8 * g + 2 * k].astype(f32)
            odd = lat_ref[8 * g + 2 * k + 1].astype(f32)
            detail = (odd - even).astype(bf16)
            wide = detail.astype(f32)
            detail_ref[4 * g + k] = detail
            head_ref[4 * g + k] = wide[:, :WIDTH].astype(bf16)
            tail_ref[4 * g + k] = wide[:, WIDTH:].astype(bf16)
            low.append((even + 0.5 * wide).astype(bf16).astype(f32))
        a, b, c, d = low
        left = (b - a).astype(bf16)
        smooth_left = (a + 0.5 * left.astype(f32)).astype(bf16).astype(f32)
        right = (d - c).astype(bf16)
        smooth_right = (c + 0.5 * right.astype(f32)).astype(bf16).astype(f32)
        top = (smooth_right - smooth_left).astype(bf16)
        lifted_ref[4 * g] = (smooth_left + 0.5 * top.astype(f32)).astype(bf16)
        lifted_ref[4 * g + 1] = left
        lifted_ref[4 * g + 2] = top
        lifted_ref[4 * g + 3] = right
        return carry

    lax.fori_loop(0, lat_ref.shape[0] // 8, group, 0)


def lift(latents):
    half = latents.shape[0] // 2
    shape = jax.ShapeDtypeStruct((half, CHANNELS, TILE), bf16)
    edge = jax.ShapeDtypeStruct((half, CHANNELS, WIDTH), bf16)
    return pl.pallas_call(
        lift_kernel,
        out_shape=[shape, edge, edge, shape],
        in_specs=[VMEM],
        out_specs=[VMEM] * 4,
        name="lift",
        compiler_params=pltpu.CompilerParams(vmem_limit_bytes=32 * MIB),
    )(latents)


def expand_matrix():
    m = np.zeros((32, 256), np.float32)
    for lane in range(128):
        slot, q = divmod(lane, 32)
        if q >= 16:
            m[q - 16, lane] = 1.0
            m[16 + slot, 128 + lane] = 1.0
    return jnp.asarray(m, bf16)


def pick_matrix(offset):
    m = np.zeros((64, 128), np.float32)
    for slot in range(4):
        for c in range(16):
            m[slot * 16 + c, slot * 32 + offset + c] = 1.0
    return jnp.asarray(m, bf16)


def put_rows(codes_ref, rows_ref, smem, sem):
    rows_ref[...] = codes_ref[...] & (ROWS - 1)
    copies = [pltpu.make_async_copy(rows_ref.at[u], smem[u], sem.at[u]) for u in range(LINES)]
    for c in copies:
        c.start()
    return copies


def place_values(values, codes_line, expand, vals_ref, u):
    slot = codes_line >> 14
    which = lax.broadcasted_iota(jnp.int32, (16, TILE), 0)
    onehot = (which == slot).astype(f32).astype(bf16)
    both = jnp.concatenate([values, onehot], axis=0)
    wide = tn(both, expand)
    start = pl.multiple_of(u * TILE, 8)
    vals_ref[pl.ds(start, TILE), :] = wide[:, :128] * wide[:, 128:]


def looked_up(vals_ref, codes_line, pick, u):
    start = pl.multiple_of(u * TILE, 8)
    rows = vals_ref[pl.ds(start, TILE), :].astype(bf16)
    parts = nt(pick, rows)
    slot = codes_line >> 14
    out = jnp.zeros((16, TILE), f32)
    for s in range(4):
        out = jnp.where(slot == s, parts[s * 16 : (s + 1) * 16], out)
    return out


def walk(smem, vals_ref, tables):
    def step(g, carry):
        for base in range(0, LINES, TABLES):
            at = [smem[base + t][g] for t in range(TABLES)]
            rows = [tables[t][pl.ds(at[t], 1), :] for t in range(TABLES)]
            adds = [vals_ref[pl.ds((base + t) * TILE + g, 1), :] for t in range(TABLES)]
            for t in range(TABLES):
                vals_ref[pl.ds((base + t) * TILE + g, 1), :] = rows[t]
                tables[t][pl.ds(at[t], 1), :] = rows[t] + adds[t]
        return carry

    lax.fori_loop(0, TILE, step, 0)


def sum_lanes(shape):
    return (lax.broadcasted_iota(jnp.int32, shape, 1) & 16) != 0


def fine_kernel(detail_ref, before_ref, after_ref, weights_ref, codebook_ref, codes_ref, expand_ref, pick_ref,
                error_ref, table_out, t0, t1, t2, t3, vals_ref, enc_ref, rows_ref, *rest):
    smem, (sem, out_sem) = rest[:LINES], rest[LINES:]
    tables = [t0, t1, t2, t3]
    copies = put_rows(codes_ref, rows_ref, smem, sem)

    eye = (lax.broadcasted_iota(jnp.int32, (256, 256), 0) == lax.broadcasted_iota(jnp.int32, (256, 256), 1))
    eye = eye.astype(f32).astype(bf16)
    blank = jnp.zeros((16, 256), bf16)

    def build(i, carry):
        pieces = []
        for h in range(2):
            start = pl.multiple_of(i * 512 + h * 256, 256)
            for s in range(4):
                pieces += [codebook_ref[:, pl.ds(s * ROWS + start, 256)], blank]
        block = nt(eye, jnp.concatenate(pieces, axis=0))
        for h in range(2):
            start = pl.multiple_of(i * 512 + h * 256, 256)
            for t in tables:
                t[pl.ds(start, 256), :] = block[:, 128 * h : 128 * h + 128]
        return carry

    lax.fori_loop(0, ROWS // 512, build, 0)

    weights = weights_ref[...]
    expand = expand_ref[...]
    column = lax.broadcasted_iota(jnp.int32, (16, 960), 1) % WIDTH

    def encode(u, carry):
        tile = detail_ref[u].astype(f32)
        ext = jnp.concatenate([before_ref[u].astype(f32), tile, after_ref[u].astype(f32)], axis=1)
        zero = jnp.zeros((16, 1), f32)
        left = jnp.where(column > 0, jnp.concatenate([zero, ext[:, :-1]], axis=1), 0.0)
        right = jnp.where(column < WIDTH - 1, jnp.concatenate([ext[:, 1:], zero], axis=1), 0.0)
        pieces = []
        for r in range(3):
            for moved in (left, ext, right):
                pieces.append(moved[:, r * WIDTH : r * WIDTH + TILE].astype(bf16))
        stacked = jnp.concatenate(pieces, axis=0)
        enc = tile + jnp.dot(weights, stacked, preferred_element_type=f32)
        enc_ref[u] = enc
        place_values(enc.astype(bf16), codes_ref[pl.ds(u, 1), :], expand, vals_ref, u)
        return carry

    lax.fori_loop(0, LINES, encode, 0)
    for c in copies:
        c.wait()
    walk(smem, vals_ref, tables)

    keep = sum_lanes((64, 128))

    def total(i, carry):
        at = pl.ds(pl.multiple_of(i * 64, 64), 64)
        t0[at, :] += jnp.where(keep, t1[at, :] + t2[at, :] + t3[at, :], 0.0)
        return carry

    lax.fori_loop(0, ROWS // 64, total, 0)
    out = pltpu.make_async_copy(t0, table_out, out_sem)
    out.start()
    pick = pick_ref[...]

    def finish(u, carry):
        looked = looked_up(vals_ref, codes_ref[pl.ds(u, 1), :], pick, u)
        error_ref[u] = (enc_ref[u] - looked).astype(bf16)
        return carry

    lax.fori_loop(0, LINES, finish, 0)
    out.wait()


def fine(detail, before, after, weights, codebook, codes):
    return pl.pallas_call(
        fine_kernel,
        out_shape=[jax.ShapeDtypeStruct((LINES, CHANNELS, TILE), bf16), jax.ShapeDtypeStruct((ROWS, 128), f32)],
        in_specs=[VMEM] * 8,
        out_specs=[VMEM, HBM],
        scratch_shapes=[pltpu.VMEM((ROWS, 128), f32)] * TABLES
        + [pltpu.VMEM((LINES * TILE, 128), f32), pltpu.VMEM((LINES, CHANNELS, TILE), f32), pltpu.VMEM((LINES, TILE), jnp.int32)]
        + [pltpu.SMEM((TILE,), jnp.int32)] * LINES
        + [pltpu.SemaphoreType.DMA((LINES,)), pltpu.SemaphoreType.DMA],
        name="fine",
        compiler_params=pltpu.CompilerParams(vmem_limit_bytes=58 * MIB),
        cost_estimate=pl.CostEstimate(flops=10**9, bytes_accessed=60 * 10**6, transcendentals=0),
    )(detail, before, after, weights, codebook, codes, expand_matrix(), pick_matrix(0))


def coarse_kernel(values_ref, codes_ref, table_in, expand_ref, pick_ref, pick_sum_ref,
                  error_ref, keep_ref, send_ref, t0, t1, t2, t3, vals_ref, rows_ref, *rest):
    smem, (sem, in_sem) = rest[:LINES], rest[LINES:]
    tables = [t0, t1, t2, t3]
    fetch = pltpu.make_async_copy(table_in, t0, in_sem)
    fetch.start()
    copies = put_rows(codes_ref, rows_ref, smem, sem)
    expand = expand_ref[...]

    def place(u, carry):
        place_values(values_ref[u], codes_ref[pl.ds(u, 1), :], expand, vals_ref, u)
        return carry

    lax.fori_loop(0, LINES, place, 0)
    fetch.wait()
    keep = sum_lanes((64, 128))

    def spread(i, carry):
        at = pl.ds(pl.multiple_of(i * 64, 64), 64)
        code_part = jnp.where(keep, 0.0, t0[at, :])
        for t in tables[1:]:
            t[at, :] = code_part
        return carry

    lax.fori_loop(0, ROWS // 64, spread, 0)
    for c in copies:
        c.wait()
    walk(smem, vals_ref, tables)
    pick_sum = pick_sum_ref[...]
    my_x, my_y, my_z, my_core = (lax.axis_index(a) for a in ("x", Y, "z", "core"))

    def total(b, carry):
        at = pl.ds(pl.multiple_of(b * 256, 256), 256)
        summed = t0[at, :] + t1[at, :] + t2[at, :] + t3[at, :]
        parts = nt(pick_sum, summed.astype(bf16)).astype(bf16)
        for s in range(4):
            place = ((s - my_x) & 3, ((b >> 4) - my_y) & 3, ((b >> 1) - my_z) & 7)
            block = parts[s * 16 : (s + 1) * 16]

            @pl.when((b & 1) == my_core)
            def _():
                keep_ref[place] = block

            @pl.when((b & 1) != my_core)
            def _():
                send_ref[place] = block

        return carry

    lax.fori_loop(0, ROWS // 256, total, 0)
    pick = pick_ref[...]
    for q in range(LINES // 4):
        parts = []
        for k in range(4):
            u = 4 * q + k
            looked = looked_up(vals_ref, codes_ref[u : u + 1, :], pick, u)
            parts.append(values_ref[u].astype(f32) - looked)
        error_ref[0, :, q * 4 * TILE : (q + 1) * 4 * TILE] = jnp.concatenate(parts, axis=1).astype(bf16)


def coarse(values, codes, table):
    return pl.pallas_call(
        coarse_kernel,
        out_shape=[jax.ShapeDtypeStruct((1, CHANNELS, LINES * TILE), bf16),
                   jax.ShapeDtypeStruct((4, 4, 8, CHANNELS, 256), bf16),
                   jax.ShapeDtypeStruct((4, 4, 8, CHANNELS, 256), bf16)],
        in_specs=[VMEM, VMEM, HBM, VMEM, VMEM, VMEM],
        out_specs=[VMEM, VMEM, VMEM],
        scratch_shapes=[pltpu.VMEM((ROWS, 128), f32)] * TABLES
        + [pltpu.VMEM((LINES * TILE, 128), f32), pltpu.VMEM((LINES, TILE), jnp.int32)]
        + [pltpu.SMEM((TILE,), jnp.int32)] * LINES
        + [pltpu.SemaphoreType.DMA((LINES,)), pltpu.SemaphoreType.DMA],
        name="coarse",
        compiler_params=pltpu.CompilerParams(vmem_limit_bytes=58 * MIB),
        cost_estimate=pl.CostEstimate(flops=10**9, bytes_accessed=60 * 10**6, transcendentals=0),
    )(values, codes, table, expand_matrix(), pick_matrix(0), pick_matrix(16))


def shift(value, axis, size, by):
    return lax.ppermute(value, axis, [(i, (i + by) % size) for i in range(size)])


def split_kernel(keep_ref, other_ref, *outs):
    upper, lower = outs[:4], outs[4:]
    def plane(z, carry):
        for x in range(4):
            for y in range(4):
                total = keep_ref[x, y, z].astype(f32) + other_ref[x, y, z].astype(f32)
                upper[y][x, z] = total[:8].astype(upper[y].dtype)
                lower[x][y, z] = total[8:].astype(lower[x].dtype)
        return carry
    lax.fori_loop(0, 8, plane, 0)


def split_first(keep, other):
    def shape(k): return jax.ShapeDtypeStruct((4, 8, 8, 256), f32 if k == 0 else bf16)
    return pl.pallas_call(split_kernel, out_shape=[shape(k) for k in range(4)] * 2, in_specs=[VMEM] * 2, out_specs=[VMEM] * 8,
        name="split_first", compiler_params=pltpu.CompilerParams(vmem_limit_bytes=32 * MIB))(keep, other)


def again_kernel(*refs):
    ins, outs = refs[:8], refs[8:]
    for half in range(2):
        own, got = ins[4 * half], ins[4 * half + 1 : 4 * half + 4]
        def plane(z, carry):
            for k in range(4):
                total = own[k, z]
                for g in got:
                    total = total + g[k, z].astype(f32)
                out = outs[4 * half + k]
                out[z] = total.astype(out.dtype)
            return carry
        lax.fori_loop(0, 8, plane, 0)


def split_again(upper, lower):
    def shape(k): return jax.ShapeDtypeStruct((8, 8, 256), f32 if k == 0 else bf16)
    return pl.pallas_call(again_kernel, out_shape=[shape(k) for k in range(4)] * 2, in_specs=[VMEM] * 8, out_specs=[VMEM] * 8,
        name="split_again", compiler_params=pltpu.CompilerParams(vmem_limit_bytes=32 * MIB))(*upper, *lower)


def last_kernel(*refs):
    ins, outs = refs[:8], refs[8:]
    for z in range(8):
        halves = []
        for half in range(2):
            total = ins[4 * half][z]
            for g in ins[4 * half + 1 : 4 * half + 4]:
                total = total + g[z].astype(f32)
            halves.append(total)
        outs[z][...] = jnp.concatenate(halves, axis=0).astype(outs[z].dtype)


def split_last(upper, lower):
    def shape(k): return jax.ShapeDtypeStruct((16, 256), f32 if k == 0 else bf16)
    return pl.pallas_call(last_kernel, out_shape=[shape(k) for k in range(8)], in_specs=[VMEM] * 8, out_specs=[VMEM] * 8,
        name="split_last", compiler_params=pltpu.CompilerParams(vmem_limit_bytes=32 * MIB))(*upper, *lower)


def join_kernel(*refs):
    total = refs[0][...]
    for g in refs[1:8]:
        total = total + g[...].astype(f32)
    refs[8][...] = total


def join(parts):
    return pl.pallas_call(join_kernel, out_shape=jax.ShapeDtypeStruct((16, 256), f32), in_specs=[VMEM] * 8, out_specs=VMEM, name="join")(*parts)


def shared_sums(keep, send):
    other = shift(send, "core", 2, 1)
    p = split_first(keep, other)
    up = [p[0]] + [shift(p[k], Y, 4, k) for k in (1, 2, 3)]
    low = [p[4]] + [shift(p[4 + k], "x", 4, k) for k in (1, 2, 3)]
    p = split_again(up, low)
    up = [p[0]] + [shift(p[k], "x", 4, k) for k in (1, 2, 3)]
    low = [p[4]] + [shift(p[4 + k], Y, 4, k) for k in (1, 2, 3)]
    p = split_last(up, low)
    return join([p[0]] + [shift(p[k], "z", 8, k) for k in range(1, 8)])


def shards(latents, conv_kernel, codebook, fine_codes, coarse_codes):
    detail, head, tail, lifted = lift(latents)
    size = lax.axis_size(SPACE)
    up = [(i, i + 1) for i in range(size - 1)]
    before = lax.ppermute(tail, SPACE, up)
    after = lax.ppermute(head, SPACE, [(j, i) for i, j in up])
    moved = lax.all_to_all(lifted, SPACE, split_axis=0, concat_axis=0, tiled=True)
    fine_error, table = fine(detail, before, after, conv_kernel, codebook, fine_codes)
    coarse_error, keep, send = coarse(moved, coarse_codes.reshape(LINES, TILE), table)
    return fine_error, coarse_error, shared_sums(keep, send)


def solution(mesh):
    split = Mesh(mesh.devices.reshape(4, 2, 2, 8, 2), CORES)
    return jax.shard_map(
        shards,
        mesh=split,
        in_specs=(P(FRAMES_BY, None, SPACE), P(), P(), P(FRAMES_BY, SPACE), P(CORES, None)),
        out_specs=(P(FRAMES_BY, None, SPACE), P(CORES, None, None), P(None, CORES)),
        check_vma=False,
    )
```

```python
import functools

import jax
import jax.numpy as jnp
import numpy as np
from jax import lax
from jax.experimental import pallas as pl
from jax.experimental.pallas import tpu as pltpu
from jax.sharding import Mesh, PartitionSpec as P

CHANNELS = 16
CODES = 65536
WIDTH = 240
TILE = 480
ROW = 256
LINE = 512
LINES = 32
ROWS = CODES // 4
TABLES = 4
MIB = 2**20
f32, bf16 = jnp.float32, jnp.bfloat16

SPACE = ("yl", "z", "core")
FRAMES_BY = ("x", "yh")
Y = ("yh", "yl")
CORES = ("x", "yh", "yl", "z", "core")

VMEM = pl.BlockSpec(memory_space=pltpu.VMEM)
HBM = pl.BlockSpec(memory_space=pl.ANY)


def nt(a, b):
    return lax.dot_general(a, b, (((1,), (1,)), ((), ())), preferred_element_type=f32)


def lift_kernel(lat_ref, head_ref, tail_ref, lifted_ref):
    gap = jnp.zeros((CHANNELS, ROW - WIDTH), f32)

    def group(g, carry):
        low = []
        for k in range(4):
            even = lat_ref[8 * g + 2 * k].astype(f32)
            odd = lat_ref[8 * g + 2 * k + 1].astype(f32)
            wide = (odd - even).astype(bf16).astype(f32)
            head_ref[4 * g + k] = jnp.concatenate([wide[:, :WIDTH], gap], axis=1).astype(bf16)
            tail_ref[4 * g + k] = jnp.concatenate([wide[:, WIDTH:], gap], axis=1).astype(bf16)
            low.append((even + 0.5 * wide).astype(bf16).astype(f32))
        a, b, c, d = low
        left = (b - a).astype(bf16)
        smooth_left = (a + 0.5 * left.astype(f32)).astype(bf16).astype(f32)
        right = (d - c).astype(bf16)
        smooth_right = (c + 0.5 * right.astype(f32)).astype(bf16).astype(f32)
        top = (smooth_right - smooth_left).astype(bf16)
        lifted_ref[4 * g] = (smooth_left + 0.5 * top.astype(f32)).astype(bf16)
        lifted_ref[4 * g + 1] = left
        lifted_ref[4 * g + 2] = top
        lifted_ref[4 * g + 3] = right
        return carry

    for g in range(lat_ref.shape[0] // 8):
        group(g, 0)


def lift(latents):
    half = latents.shape[0] // 2
    shape = jax.ShapeDtypeStruct((half, CHANNELS, TILE), bf16)
    edge = jax.ShapeDtypeStruct((half, CHANNELS, ROW), bf16)
    return pl.pallas_call(
        lift_kernel,
        out_shape=[edge, edge, shape],
        grid=(4,),
        in_specs=[pl.BlockSpec((half // 2, CHANNELS, TILE), lambda i: (i, 0, 0))],
        out_specs=[pl.BlockSpec((half // 4, CHANNELS, n), lambda i: (i, 0, 0)) for n in (ROW, ROW, TILE)],
        name="lift",
        compiler_params=pltpu.CompilerParams(vmem_limit_bytes=60 * MIB),
    )(latents)


def identity():
    return jnp.asarray(np.eye(256), bf16)


def table_kernel(codebook_ref, eye_ref, table_ref):
    blank = jnp.zeros((16, 256), bf16)
    for k in range(4):
        pieces = []
        for h in range(2):
            start = pl.multiple_of(pl.program_id(0) * 2048 + k * 512 + h * 256, 256)
            for s in range(4):
                pieces += [codebook_ref[:, pl.ds(s * ROWS + start, 256)], blank]
        block = nt(eye_ref[...], jnp.concatenate(pieces, axis=0))
        table_ref[k * 512 : k * 512 + 256, :] = block[:, :128]
        table_ref[k * 512 + 256 : k * 512 + 512, :] = block[:, 128:]


def code_table(codebook):
    return pl.pallas_call(
        table_kernel,
        grid=(ROWS // 2048,),
        out_shape=jax.ShapeDtypeStruct((ROWS, 128), f32),
        in_specs=[pl.BlockSpec((CHANNELS, CODES), lambda i: (0, 0)), pl.BlockSpec((256, 256), lambda i: (0, 0))],
        out_specs=pl.BlockSpec((2048, 128), lambda i: (i, 0)),
        name="code_table",
        compiler_params=pltpu.CompilerParams(vmem_limit_bytes=60 * MIB),
        cost_estimate=pl.CostEstimate(flops=10**9, bytes_accessed=10**7, transcendentals=0),
    )(codebook, identity())


def pick_matrix(offset):
    m = np.zeros((64, 128), np.float32)
    for slot in range(4):
        for c in range(16):
            m[slot * 16 + c, slot * 32 + offset + c] = 1.0
    return jnp.asarray(m, bf16)


def put_rows(codes, rows_ref, smem, sem):
    rows_ref[...] = codes & (ROWS - 1)
    copies = [pltpu.make_async_copy(rows_ref.at[u], smem[u], sem.at[u]) for u in range(LINES)]
    for c in copies:
        c.start()
    return copies


def slotted(values, codes_line):
    slot = codes_line >> 14
    blank = jnp.zeros((16, LINE), f32)
    pieces = []
    for s in range(4):
        pieces += [blank, jnp.where(slot == s, values, 0.0)]
    return jnp.concatenate(pieces, axis=0).astype(bf16)


def place_pair(first, second, eye, vals_ref, u):
    for h in range(2):
        at = slice(256 * h, 256 * h + 256)
        block = nt(eye, jnp.concatenate([first[:, at], second[:, at]], axis=0))
        for k in range(2):
            start = pl.multiple_of((u + k) * LINE + 256 * h, 256)
            vals_ref[pl.ds(start, 256), :] = block[:, 128 * k : 128 * k + 128]


def looked_up(vals_ref, codes_line, pick, u):
    start = pl.multiple_of(u * LINE, LINE)
    rows = vals_ref[pl.ds(start, LINE), :].astype(bf16)
    parts = nt(pick, rows)
    slot = codes_line >> 14
    out = parts[:16]
    for s in range(1, 4):
        out = jnp.where(slot == s, parts[s * 16 : (s + 1) * 16], out)
    return out


def walk(smem, vals_ref, tables, start, stop):
    def step(g, carry):
        for base in range(0, LINES, TABLES):
            at = [smem[base + t][g] for t in range(TABLES)]
            rows = [tables[t][pl.ds(at[t], 1), :] for t in range(TABLES)]
            adds = [vals_ref[pl.ds((base + t) * LINE + g, 1), :] for t in range(TABLES)]
            for t in range(TABLES):
                vals_ref[pl.ds((base + t) * LINE + g, 1), :] = rows[t]
                tables[t][pl.ds(at[t], 1), :] = rows[t] + adds[t]
        return carry

    lax.fori_loop(start, stop, step, 0)


def quantize_kernel(before_ref, head_ref, tail_ref, after_ref, values_ref, weights_ref, fine_codes_ref, coarse_codes_ref,
                    eye_ref, pick_ref, pick_sum_ref, table_in, fine_error_ref, coarse_error_ref, keep_ref, send_ref,
                    t0, t1, t2, t3, vals_ref, enc_ref, fine_padded, coarse_padded, fine_rows, coarse_rows, *rest):
    fine_smem, coarse_smem, (fine_sem, coarse_sem, in_sem) = rest[:LINES], rest[LINES : 2 * LINES], rest[2 * LINES :]
    tables = [t0, t1, t2, t3]
    fetch = pltpu.make_async_copy(table_in, t0, in_sem)
    fetch.start()
    gap = jnp.zeros((LINES, ROW - WIDTH), jnp.int32)
    fine_padded[...] = jnp.concatenate([fine_codes_ref[:, :WIDTH], gap, fine_codes_ref[:, WIDTH:], gap], axis=1)
    fine_copies = put_rows(fine_padded[...], fine_rows, fine_smem, fine_sem)
    gap = jnp.zeros((1, LINE - TILE), jnp.int32)
    for u in range(LINES):
        coarse_padded[u : u + 1, :] = jnp.concatenate([coarse_codes_ref[:, u * TILE : (u + 1) * TILE], gap], axis=1)
    coarse_copies = put_rows(coarse_padded[...], coarse_rows, coarse_smem, coarse_sem)
    weights, eye, pick, pick_sum = weights_ref[...], eye_ref[...], pick_ref[...], pick_sum_ref[...]

    def encoded(u):
        lines = [r[u].astype(f32) for r in (before_ref, head_ref, tail_ref, after_ref)]
        moved = [[pltpu.roll(v, 1, 1) for v in lines], lines, [pltpu.roll(v, ROW - 1, 1) for v in lines]]
        pieces = []
        for r in range(3):
            for m in moved:
                pieces.append(jnp.concatenate([m[r], m[r + 1]], axis=1).astype(bf16))
        stacked = jnp.concatenate(pieces, axis=0)
        enc = jnp.concatenate([lines[1], lines[2]], axis=1) + jnp.dot(weights, stacked, preferred_element_type=f32)
        enc_ref[u] = enc
        return slotted(enc, fine_padded[pl.ds(u, 1), :])

    def encode(p, carry):
        for k in range(2):
            u = 4 * p + 2 * k
            place_pair(encoded(u), encoded(u + 1), eye, vals_ref, u)
        return carry

    lax.fori_loop(0, LINES // 4, encode, 0)
    fetch.wait()

    def spread(i, carry):
        at = pl.ds(pl.multiple_of(i * 64, 64), 64)
        code_part = t0[at, :]
        for t in tables[1:]:
            t[at, :] = code_part
        return carry

    lax.fori_loop(0, ROWS // 64, spread, 0)
    for c in fine_copies:
        c.wait()
    walk(fine_smem, vals_ref, tables, 0, WIDTH)
    walk(fine_smem, vals_ref, tables, ROW, ROW + WIDTH)

    tail_gap = jnp.zeros((CHANNELS, LINE - TILE), f32)

    def slots_of(u):
        values = jnp.concatenate([values_ref[u].astype(f32), tail_gap], axis=1)
        return slotted(values, coarse_padded[pl.ds(u, 1), :])

    def turn(p, carry):
        for k in range(4):
            u = 4 * p + k
            error = enc_ref[u] - looked_up(vals_ref, fine_padded[pl.ds(u, 1), :], pick, u)
            fine_error_ref[u] = jnp.concatenate([error[:, :WIDTH], error[:, ROW : ROW + WIDTH]], axis=1).astype(bf16)
        for k in range(2):
            u = 4 * p + 2 * k
            place_pair(slots_of(u), slots_of(u + 1), eye, vals_ref, u)
        return carry

    lax.fori_loop(0, LINES // 4, turn, 0)
    for c in coarse_copies:
        c.wait()
    walk(coarse_smem, vals_ref, tables, 0, TILE)
    my_x, my_y, my_z, my_core = (lax.axis_index(a) for a in ("x", Y, "z", "core"))

    def total(i, carry):
        for out_ref, core in ((send_ref, 1 - my_core), (keep_ref, my_core)):
            b = 2 * i + core
            at = pl.ds(pl.multiple_of(b * 256, 256), 256)
            summed = t0[at, :] + t1[at, :] + t2[at, :] + t3[at, :]
            parts = nt(pick_sum, summed.astype(bf16)).astype(bf16)
            y_off = ((b >> 4) - my_y) & 3
            z_off = ((b >> 1) & 7) ^ my_z
            z_top = z_off >> 2
            z_at = z_off ^ (3 * z_top)
            for s in range(4):
                x_off = (s - my_x) & 3
                place = (jnp.where(core == 0, x_off, y_off), jnp.where(core == 0, y_off, x_off), z_at)
                out_ref[place] = parts[s * 16 : (s + 1) * 16]
        return carry

    lax.fori_loop(0, ROWS // 512, total, 0)
    for q in range(LINES // 4):
        parts = []
        for k in range(4):
            u = 4 * q + k
            looked = looked_up(vals_ref, coarse_padded[u : u + 1, :], pick, u)
            parts.append(values_ref[u].astype(f32) - looked[:, :TILE])
        coarse_error_ref[0, :, q * 4 * TILE : (q + 1) * 4 * TILE] = jnp.concatenate(parts, axis=1).astype(bf16)


def quantize(before, head, tail, after, values, weights, fine_codes, coarse_codes, table):
    sums = jax.ShapeDtypeStruct((4, 4, 8, CHANNELS, 256), bf16)
    return pl.pallas_call(
        quantize_kernel,
        out_shape=[jax.ShapeDtypeStruct((LINES, CHANNELS, TILE), bf16),
                   jax.ShapeDtypeStruct((1, CHANNELS, LINES * TILE), bf16), sums, sums],
        in_specs=[VMEM] * 11 + [HBM],
        out_specs=[VMEM] * 4,
        scratch_shapes=[pltpu.VMEM((ROWS, 128), f32)] * TABLES
        + [pltpu.VMEM((LINES * LINE, 128), f32), pltpu.VMEM((LINES, CHANNELS, LINE), f32)]
        + [pltpu.VMEM((LINES, LINE), jnp.int32)] * 4
        + [pltpu.SMEM((LINE,), jnp.int32)] * (2 * LINES)
        + [pltpu.SemaphoreType.DMA((LINES,)), pltpu.SemaphoreType.DMA((LINES,)), pltpu.SemaphoreType.DMA],
        name="quantize",
        compiler_params=pltpu.CompilerParams(vmem_limit_bytes=58 * MIB),
        cost_estimate=pl.CostEstimate(flops=10**9, bytes_accessed=10**8, transcendentals=0),
    )(before, head, tail, after, values, weights, fine_codes, coarse_codes, identity(), pick_matrix(0), pick_matrix(16), table)


def device_of(x, y, z, core):
    return ((x % 4 * 4 + y % 4) * 8 + z) * 2 + core


def permuted(value, target):
    pairs = [(device_of(x, y, z, c), device_of(*target(x, y, z, c)))
             for x in range(4) for y in range(4) for z in range(8) for c in range(2)]
    return lax.ppermute(value, CORES, pairs)


def along(first, k):
    def target(x, y, z, c):
        return (x + k, y, z, c) if (c == 0) == first else (x, y + k, z, c)
    return target


def across(bits):
    return lambda x, y, z, c: (x, y, z ^ bits, c)


def add_kernel(n_in, *refs):
    ins, outs = refs[:n_in], refs[n_in:]
    rows = ins[0].shape[0] // len(outs)

    def piece(k, i):
        total = ins[0][k * rows + i].astype(f32)
        for r in ins[1:]:
            total = total + r[k * rows + i].astype(f32)
        outs[k][i] = total.astype(outs[k].dtype)

    for k in range(len(outs)):
        if rows <= 4:
            for i in range(rows):
                piece(k, i)
        else:
            def several(j, carry, k=k):
                for i in range(4):
                    piece(k, 4 * j + i)
                return carry
            lax.fori_loop(0, rows // 4, several, 0)


def added(ways, *parts):
    share = parts[0].shape[0] // ways
    shapes = [jax.ShapeDtypeStruct((share, CHANNELS, 256), f32 if k == 0 else bf16) for k in range(ways)]
    return pl.pallas_call(
        functools.partial(add_kernel, len(parts)),
        out_shape=shapes,
        in_specs=[VMEM] * len(parts),
        out_specs=[VMEM] * ways,
        name="add",
        compiler_params=pltpu.CompilerParams(vmem_limit_bytes=16 * MIB),
    )(*parts)


def shared_sums(keep, send):
    keep, send = (v.reshape(128, CHANNELS, 256) for v in (keep, send))
    own, *sends = added(4, keep, permuted(send, lambda x, y, z, c: (x, y, z, 1 - c)))
    for first in (True, False):
        got = [permuted(s, along(first, k + 1)) for k, s in enumerate(sends)]
        own, *sends = added(4 if first else 2, own, *got)
    for bits, ways in ((7, 2), (2, 2), (1, 1)):
        own, *sends = added(ways, own, permuted(sends[0], across(bits)))
    return own[0]


def shards(latents, conv_kernel, codebook, fine_codes, coarse_codes):
    head, tail, lifted = lift(latents)
    size = lax.axis_size(SPACE)
    up = [(i, i + 1) for i in range(size - 1)]
    before = lax.ppermute(tail, SPACE, up)
    after = lax.ppermute(head, SPACE, [(j, i) for i, j in up])
    table = code_table(codebook)
    moved = lax.all_to_all(lifted, SPACE, split_axis=0, concat_axis=0, tiled=True)
    fine_error, coarse_error, keep, send = quantize(
        before, head, tail, after, moved, conv_kernel, fine_codes, coarse_codes, table)
    return fine_error, coarse_error, shared_sums(keep, send)


def solution(mesh):
    split = Mesh(mesh.devices.reshape(4, 2, 2, 8, 2), CORES)
    return jax.shard_map(
        shards,
        mesh=split,
        in_specs=(P(FRAMES_BY, None, SPACE), P(), P(), P(FRAMES_BY, SPACE), P(CORES, None)),
        out_specs=(P(FRAMES_BY, None, SPACE), P(CORES, None, None), P(None, CORES)),
        check_vma=False,
    )
```

```python
import functools

import jax
import jax.numpy as jnp
import numpy as np
from jax import lax
from jax.experimental import pallas as pl
from jax.experimental.pallas import tpu as pltpu
from jax.sharding import Mesh, PartitionSpec as P

CHANNELS = 16
CODES = 65536
WIDTH = 240
TILE = 480
ROW = 256
LINE = 512
LINES = 32
ROWS = CODES // 4
TABLES = 4
MIB = 2**20
f32, bf16 = jnp.float32, jnp.bfloat16

SPACE = ("yl", "z", "core")
FRAMES_BY = ("x", "yh")
Y = ("yh", "yl")
CORES = ("x", "yh", "yl", "z", "core")

VMEM = pl.BlockSpec(memory_space=pltpu.VMEM)
HBM = pl.BlockSpec(memory_space=pl.ANY)


def nt(a, b):
    return lax.dot_general(a, b, (((1,), (1,)), ((), ())), preferred_element_type=f32)


def lift_kernel(lat_ref, head_ref, tail_ref, lifted_ref):
    gap = jnp.zeros((CHANNELS, ROW - WIDTH), f32)

    def group(g, carry):
        low = []
        for k in range(4):
            even = lat_ref[8 * g + 2 * k].astype(f32)
            odd = lat_ref[8 * g + 2 * k + 1].astype(f32)
            wide = (odd - even).astype(bf16).astype(f32)
            head_ref[4 * g + k] = jnp.concatenate([wide[:, :WIDTH], gap], axis=1).astype(bf16)
            tail_ref[4 * g + k] = jnp.concatenate([wide[:, WIDTH:], gap], axis=1).astype(bf16)
            low.append((even + 0.5 * wide).astype(bf16).astype(f32))
        a, b, c, d = low
        left = (b - a).astype(bf16)
        smooth_left = (a + 0.5 * left.astype(f32)).astype(bf16).astype(f32)
        right = (d - c).astype(bf16)
        smooth_right = (c + 0.5 * right.astype(f32)).astype(bf16).astype(f32)
        top = (smooth_right - smooth_left).astype(bf16)
        lifted_ref[4 * g] = (smooth_left + 0.5 * top.astype(f32)).astype(bf16)
        lifted_ref[4 * g + 1] = left
        lifted_ref[4 * g + 2] = top
        lifted_ref[4 * g + 3] = right
        return carry

    for g in range(lat_ref.shape[0] // 8):
        group(g, 0)


def lift(latents):
    half = latents.shape[0] // 2
    shape = jax.ShapeDtypeStruct((half, CHANNELS, TILE), bf16)
    edge = jax.ShapeDtypeStruct((half, CHANNELS, ROW), bf16)
    return pl.pallas_call(
        lift_kernel,
        out_shape=[edge, edge, shape],
        grid=(2,),
        in_specs=[pl.BlockSpec((half, CHANNELS, TILE), lambda i: (i, 0, 0))],
        out_specs=[pl.BlockSpec((half // 2, CHANNELS, n), lambda i: (i, 0, 0)) for n in (ROW, ROW, TILE)],
        name="lift",
        compiler_params=pltpu.CompilerParams(vmem_limit_bytes=60 * MIB),
    )(latents)


def identity():
    return jnp.asarray(np.eye(256), bf16)


def table_kernel(codebook_ref, eye_ref, table_ref):
    blank = jnp.zeros((16, 256), bf16)
    for k in range(4):
        pieces = []
        for h in range(2):
            start = pl.multiple_of(pl.program_id(0) * 2048 + k * 512 + h * 256, 256)
            for s in range(4):
                pieces += [codebook_ref[:, pl.ds(s * ROWS + start, 256)], blank]
        block = nt(eye_ref[...], jnp.concatenate(pieces, axis=0))
        table_ref[k * 512 : k * 512 + 256, :] = block[:, :128]
        table_ref[k * 512 + 256 : k * 512 + 512, :] = block[:, 128:]


def code_table(codebook):
    return pl.pallas_call(
        table_kernel,
        grid=(ROWS // 2048,),
        out_shape=jax.ShapeDtypeStruct((ROWS, 128), f32),
        in_specs=[pl.BlockSpec((CHANNELS, CODES), lambda i: (0, 0)), pl.BlockSpec((256, 256), lambda i: (0, 0))],
        out_specs=pl.BlockSpec((2048, 128), lambda i: (i, 0)),
        name="code_table",
        compiler_params=pltpu.CompilerParams(vmem_limit_bytes=60 * MIB),
        cost_estimate=pl.CostEstimate(flops=10**9, bytes_accessed=10**7, transcendentals=0),
    )(codebook, identity())


def pick_matrix(offset):
    m = np.zeros((64, 128), np.float32)
    for slot in range(4):
        for c in range(16):
            m[slot * 16 + c, slot * 32 + offset + c] = 1.0
    return jnp.asarray(m, bf16)


def put_rows(codes, rows_ref, smem, sem):
    rows_ref[...] = codes & (ROWS - 1)
    copies = [pltpu.make_async_copy(rows_ref.at[u], smem[u], sem.at[u]) for u in range(LINES)]
    for c in copies:
        c.start()
    return copies


def slotted(values, slot):
    return [jnp.where(slot == s, values, 0.0) for s in range(4)]


def spaced(pieces):
    blank = jnp.zeros((16, LINE), bf16)
    return jnp.concatenate([v for p in pieces for v in (blank, p.astype(bf16))], axis=0)


def vals_rows(group, k, start, count):
    return pl.ds((group * LINE + start) * 8 + k, count, stride=8)


def place_pair(first, second, same, eye, vals_ref, group, k):
    second = [b + jnp.where(same, a, 0.0) for a, b in zip(first, second)]
    first, second = spaced(first), spaced(second)
    for h in range(2):
        at = slice(256 * h, 256 * h + 256)
        block = nt(eye, jnp.concatenate([first[:, at], second[:, at]], axis=0))
        vals_ref[vals_rows(group, k, 256 * h, 256), :] = block[:, :128]
        vals_ref[vals_rows(group, k + 4, 256 * h, 256), :] = block[:, 128:]


def looked_up(vals_ref, slot, pick, group, k):
    rows = vals_ref[vals_rows(group, k, 0, LINE), :].astype(bf16)
    parts = nt(pick, rows)
    out = parts[:16]
    for s in range(1, 4):
        out = jnp.where(slot == s, parts[s * 16 : (s + 1) * 16], out)
    return out


def walk(smem, vals_ref, tables, start, stop):
    sub = lax.broadcasted_iota(jnp.int32, (8, 128), 0)

    def one(g):
        for group in range(LINES // 8):
            here = pl.ds(pl.multiple_of((group * LINE + g) * 8, 8), 8)
            tile = vals_ref[here, :]
            at = [pl.ds(smem[group * 8 + k][g] + (8 - k), 8) for k in range(8)]
            rows = [tables[k % TABLES][at[k], :] for k in range(8)]
            for k in range(8):
                pltpu.store(tables[k % TABLES].at[at[k], :], rows[k] + tile, mask=sub == k)
            out = rows[0]
            for k in range(1, 8):
                out = jnp.where(sub == k, rows[k], out)
            vals_ref[here, :] = out

    def step(i, carry):
        one(start + 2 * i)
        one(start + 2 * i + 1)
        return carry

    lax.fori_loop(0, (stop - start) // 2, step, 0)


def quantize_kernel(before_ref, head_ref, tail_ref, after_ref, values_ref, weights_ref, fine_codes_ref, coarse_codes_ref,
                    eye_ref, pick_ref, pick_sum_ref, table_in, fine_error_ref, coarse_error_ref, keep_ref, send_ref,
                    t0, t1, t2, t3, vals_ref, enc_ref, fine_padded, coarse_padded, fine_rows, coarse_rows, *rest):
    fine_smem, coarse_smem, (fine_sem, coarse_sem, in_sem) = rest[:LINES], rest[LINES : 2 * LINES], rest[2 * LINES :]
    tables = [t0, t1, t2, t3]
    fetch = pltpu.make_async_copy(table_in, t0.at[pl.ds(8, ROWS), :], in_sem)
    fetch.start()
    gap = jnp.zeros((LINES, ROW - WIDTH), jnp.int32)
    fine_padded[...] = jnp.concatenate([fine_codes_ref[:, :WIDTH], gap, fine_codes_ref[:, WIDTH:], gap], axis=1)
    fine_copies = put_rows(fine_padded[...], fine_rows, fine_smem, fine_sem)
    gap = jnp.zeros((1, LINE - TILE), jnp.int32)
    for u in range(LINES):
        coarse_padded[u : u + 1, :] = jnp.concatenate([coarse_codes_ref[:, u * TILE : (u + 1) * TILE], gap], axis=1)
    coarse_copies = put_rows(coarse_padded[...], coarse_rows, coarse_smem, coarse_sem)
    weights, eye, pick, pick_sum = weights_ref[...], eye_ref[...], pick_ref[...], pick_sum_ref[...]

    def encoded(u):
        lines = [r[u].astype(f32) for r in (before_ref, head_ref, tail_ref, after_ref)]
        moved = [[pltpu.roll(v, 1, 1) for v in lines], lines, [pltpu.roll(v, ROW - 1, 1) for v in lines]]
        pieces = []
        for r in range(3):
            for m in moved:
                pieces.append(jnp.concatenate([m[r], m[r + 1]], axis=1).astype(bf16))
        stacked = jnp.concatenate(pieces, axis=0)
        enc = jnp.concatenate([lines[1], lines[2]], axis=1) + jnp.dot(weights, stacked, preferred_element_type=f32)
        enc_ref[u] = enc
        return slotted(enc, fine_padded[pl.ds(u, 1), :] >> 14)

    def encode(group, carry):
        for k in range(4):
            u = 8 * group + k
            same = fine_rows[pl.ds(u, 1), :] == fine_rows[pl.ds(u + 4, 1), :]
            place_pair(encoded(u), encoded(u + 4), same, eye, vals_ref, group, k)
        return carry

    lax.fori_loop(0, LINES // 8, encode, 0)
    fetch.wait()

    def spread(i, carry):
        at = pl.ds(pl.multiple_of(i * 64 + 8, 8), 64)
        code_part = t0[at, :]
        for t in tables[1:]:
            t[at, :] = code_part
        return carry

    lax.fori_loop(0, ROWS // 64, spread, 0)
    for c in fine_copies:
        c.wait()
    walk(fine_smem, vals_ref, tables, 0, WIDTH)
    walk(fine_smem, vals_ref, tables, ROW, ROW + WIDTH)

    tail_gap = jnp.zeros((CHANNELS, LINE - TILE), f32)

    def slots_of(u):
        values = jnp.concatenate([values_ref[u].astype(f32), tail_gap], axis=1)
        return slotted(values, coarse_padded[pl.ds(u, 1), :] >> 14)

    def turn(group, carry):
        for k in range(8):
            u = 8 * group + k
            error = enc_ref[u] - looked_up(vals_ref, fine_padded[pl.ds(u, 1), :] >> 14, pick, group, k)
            fine_error_ref[u] = jnp.concatenate([error[:, :WIDTH], error[:, ROW : ROW + WIDTH]], axis=1).astype(bf16)
        for k in range(4):
            u = 8 * group + k
            same = coarse_rows[pl.ds(u, 1), :] == coarse_rows[pl.ds(u + 4, 1), :]
            place_pair(slots_of(u), slots_of(u + 4), same, eye, vals_ref, group, k)
        return carry

    lax.fori_loop(0, LINES // 8, turn, 0)
    for c in coarse_copies:
        c.wait()
    walk(coarse_smem, vals_ref, tables, 0, TILE)
    my_x, my_y, my_z, my_core = (lax.axis_index(a) for a in ("x", Y, "z", "core"))

    def total(i, carry):
        for out_ref, core in ((send_ref, 1 - my_core), (keep_ref, my_core)):
            b = 2 * i + core
            at = pl.ds(pl.multiple_of(b * 256 + 8, 8), 256)
            summed = t0[at, :] + t1[at, :] + t2[at, :] + t3[at, :]
            parts = nt(pick_sum, summed.astype(bf16)).astype(bf16)
            y_off = ((b >> 4) - my_y) & 3
            z_off = ((b >> 1) & 7) ^ my_z
            z_top = z_off >> 2
            z_at = z_off ^ (3 * z_top)
            for s in range(4):
                x_off = (s - my_x) & 3
                place = (jnp.where(core == 0, x_off, y_off), jnp.where(core == 0, y_off, x_off), z_at)
                out_ref[place] = parts[s * 16 : (s + 1) * 16]
        return carry

    lax.fori_loop(0, ROWS // 512, total, 0)
    for q in range(LINES // 4):
        parts = []
        for k in range(4):
            u = 4 * q + k
            looked = looked_up(vals_ref, coarse_padded[u : u + 1, :] >> 14, pick, u // 8, u % 8)
            parts.append(values_ref[u].astype(f32) - looked[:, :TILE])
        coarse_error_ref[0, :, q * 4 * TILE : (q + 1) * 4 * TILE] = jnp.concatenate(parts, axis=1).astype(bf16)


def quantize(before, head, tail, after, values, weights, fine_codes, coarse_codes, table):
    sums = jax.ShapeDtypeStruct((4, 4, 8, CHANNELS, 256), bf16)
    return pl.pallas_call(
        quantize_kernel,
        out_shape=[jax.ShapeDtypeStruct((LINES, CHANNELS, TILE), bf16),
                   jax.ShapeDtypeStruct((1, CHANNELS, LINES * TILE), bf16), sums, sums],
        in_specs=[VMEM] * 11 + [HBM],
        out_specs=[VMEM] * 4,
        scratch_shapes=[pltpu.VMEM((ROWS + 16, 128), f32)] * TABLES
        + [pltpu.VMEM((LINES * LINE, 128), f32), pltpu.VMEM((LINES, CHANNELS, LINE), f32)]
        + [pltpu.VMEM((LINES, LINE), jnp.int32)] * 4
        + [pltpu.SMEM((LINE,), jnp.int32)] * (2 * LINES)
        + [pltpu.SemaphoreType.DMA((LINES,)), pltpu.SemaphoreType.DMA((LINES,)), pltpu.SemaphoreType.DMA],
        name="quantize",
        compiler_params=pltpu.CompilerParams(vmem_limit_bytes=50 * MIB),
        cost_estimate=pl.CostEstimate(flops=10**9, bytes_accessed=10**8, transcendentals=0),
    )(before, head, tail, after, values, weights, fine_codes, coarse_codes, identity(), pick_matrix(0), pick_matrix(16), table)


def device_of(x, y, z, core):
    return ((x % 4 * 4 + y % 4) * 8 + z) * 2 + core


def permuted(value, target):
    pairs = [(device_of(x, y, z, c), device_of(*target(x, y, z, c)))
             for x in range(4) for y in range(4) for z in range(8) for c in range(2)]
    return lax.ppermute(value, CORES, pairs)


def along(first, k):
    def target(x, y, z, c):
        return (x + k, y, z, c) if (c == 0) == first else (x, y + k, z, c)
    return target


def across(bits):
    return lambda x, y, z, c: (x, y, z ^ bits, c)


def add_kernel(n_in, *refs):
    ins, outs = refs[:n_in], refs[n_in:]
    rows = ins[0].shape[0] // len(outs)

    def piece(k, i):
        total = ins[0][k * rows + i].astype(f32)
        for r in ins[1:]:
            total = total + r[k * rows + i].astype(f32)
        outs[k][i] = total.astype(outs[k].dtype)

    for k in range(len(outs)):
        if rows <= 4:
            for i in range(rows):
                piece(k, i)
        else:
            def several(j, carry, k=k):
                for i in range(4):
                    piece(k, 4 * j + i)
                return carry
            lax.fori_loop(0, rows // 4, several, 0)


def added(ways, *parts):
    share = parts[0].shape[0] // ways
    shapes = [jax.ShapeDtypeStruct((share, CHANNELS, 256), f32 if k == 0 else bf16) for k in range(ways)]
    return pl.pallas_call(
        functools.partial(add_kernel, len(parts)),
        out_shape=shapes,
        in_specs=[VMEM] * len(parts),
        out_specs=[VMEM] * ways,
        name="add",
        compiler_params=pltpu.CompilerParams(vmem_limit_bytes=16 * MIB),
    )(*parts)


def shared_sums(keep, send):
    keep, send = (v.reshape(128, CHANNELS, 256) for v in (keep, send))
    own, *sends = added(4, keep, permuted(send, lambda x, y, z, c: (x, y, z, 1 - c)))
    for first in (True, False):
        got = [permuted(s, along(first, k + 1)) for k, s in enumerate(sends)]
        own, *sends = added(4 if first else 2, own, *got)
    for bits, ways in ((7, 2), (2, 2), (1, 1)):
        own, *sends = added(ways, own, permuted(sends[0], across(bits)))
    return own[0]


def shards(latents, conv_kernel, codebook, fine_codes, coarse_codes):
    head, tail, lifted = lift(latents)
    size = lax.axis_size(SPACE)
    up = [(i, i + 1) for i in range(size - 1)]
    before = lax.ppermute(tail, SPACE, up)
    after = lax.ppermute(head, SPACE, [(j, i) for i, j in up])
    table = code_table(codebook)
    moved = lax.all_to_all(lifted, SPACE, split_axis=0, concat_axis=0, tiled=True)
    fine_error, coarse_error, keep, send = quantize(
        before, head, tail, after, moved, conv_kernel, fine_codes, coarse_codes, table)
    return fine_error, coarse_error, shared_sums(keep, send)


def solution(mesh):
    split = Mesh(mesh.devices.reshape(4, 2, 2, 8, 2), CORES)
    return jax.shard_map(
        shards,
        mesh=split,
        in_specs=(P(FRAMES_BY, None, SPACE), P(), P(), P(FRAMES_BY, SPACE), P(CORES, None)),
        out_specs=(P(FRAMES_BY, None, SPACE), P(CORES, None, None), P(None, CORES)),
        check_vma=False,
    )
```

```python
import functools

import jax
import jax.numpy as jnp
import numpy as np
from jax import lax
from jax.experimental import pallas as pl
from jax.experimental.pallas import tpu as pltpu
from jax.sharding import Mesh, PartitionSpec as P

CHANNELS = 16
CODES = 65536
WIDTH = 240
TILE = 480
ROW = 256
LINE = 512
LINES = 32
ROWS = CODES // 4
TABLES = 4
MIB = 2**20
f32, bf16 = jnp.float32, jnp.bfloat16

SPACE = ("yl", "z", "core")
FRAMES_BY = ("x", "yh")
Y = ("yh", "yl")
CORES = ("x", "yh", "yl", "z", "core")

VMEM = pl.BlockSpec(memory_space=pltpu.VMEM)
HBM = pl.BlockSpec(memory_space=pl.ANY)


def nt(a, b):
    return lax.dot_general(a, b, (((1,), (1,)), ((), ())), preferred_element_type=f32)


def lift_kernel(lat_ref, head_ref, tail_ref, lifted_ref):
    gap = jnp.zeros((CHANNELS, ROW - WIDTH), f32)

    def group(g, carry):
        low = []
        for k in range(4):
            even = lat_ref[8 * g + 2 * k].astype(f32)
            odd = lat_ref[8 * g + 2 * k + 1].astype(f32)
            wide = (odd - even).astype(bf16).astype(f32)
            head_ref[4 * g + k] = jnp.concatenate([wide[:, :WIDTH], gap], axis=1).astype(bf16)
            tail_ref[4 * g + k] = jnp.concatenate([wide[:, WIDTH:], gap], axis=1).astype(bf16)
            low.append((even + 0.5 * wide).astype(bf16).astype(f32))
        a, b, c, d = low
        left = (b - a).astype(bf16)
        smooth_left = (a + 0.5 * left.astype(f32)).astype(bf16).astype(f32)
        right = (d - c).astype(bf16)
        smooth_right = (c + 0.5 * right.astype(f32)).astype(bf16).astype(f32)
        top = (smooth_right - smooth_left).astype(bf16)
        lifted_ref[4 * g] = (smooth_left + 0.5 * top.astype(f32)).astype(bf16)
        lifted_ref[4 * g + 1] = left
        lifted_ref[4 * g + 2] = top
        lifted_ref[4 * g + 3] = right
        return carry

    for g in range(lat_ref.shape[0] // 8):
        group(g, 0)


def lift(latents):
    half = latents.shape[0] // 2
    shape = jax.ShapeDtypeStruct((half, CHANNELS, TILE), bf16)
    edge = jax.ShapeDtypeStruct((half, CHANNELS, ROW), bf16)
    return pl.pallas_call(
        lift_kernel,
        out_shape=[edge, edge, shape],
        grid=(2,),
        in_specs=[pl.BlockSpec((half, CHANNELS, TILE), lambda i: (i, 0, 0))],
        out_specs=[pl.BlockSpec((half // 2, CHANNELS, n), lambda i: (i, 0, 0)) for n in (ROW, ROW, TILE)],
        name="lift",
        compiler_params=pltpu.CompilerParams(vmem_limit_bytes=60 * MIB),
    )(latents)


def identity():
    return jnp.asarray(np.eye(256), bf16)


def table_kernel(codebook_ref, eye_ref, table_ref):
    blank = jnp.zeros((16, 256), bf16)
    for k in range(4):
        pieces = []
        for h in range(2):
            start = pl.multiple_of(pl.program_id(0) * 2048 + k * 512 + h * 256, 256)
            for s in range(4):
                pieces += [codebook_ref[:, pl.ds(s * ROWS + start, 256)], blank]
        block = nt(eye_ref[...], jnp.concatenate(pieces, axis=0))
        table_ref[k * 512 : k * 512 + 256, :] = block[:, :128]
        table_ref[k * 512 + 256 : k * 512 + 512, :] = block[:, 128:]


def code_table(codebook):
    return pl.pallas_call(
        table_kernel,
        grid=(ROWS // 2048,),
        out_shape=jax.ShapeDtypeStruct((ROWS, 128), f32),
        in_specs=[pl.BlockSpec((CHANNELS, CODES), lambda i: (0, 0)), pl.BlockSpec((256, 256), lambda i: (0, 0))],
        out_specs=pl.BlockSpec((2048, 128), lambda i: (i, 0)),
        name="code_table",
        compiler_params=pltpu.CompilerParams(vmem_limit_bytes=60 * MIB),
        cost_estimate=pl.CostEstimate(flops=10**9, bytes_accessed=10**7, transcendentals=0),
    )(codebook, identity())


def pick_matrix(offset):
    m = np.zeros((64, 128), np.float32)
    for slot in range(4):
        for c in range(16):
            m[slot * 16 + c, slot * 32 + offset + c] = 1.0
    return jnp.asarray(m, bf16)


def put_rows(codes, rows_ref, smem, sem):
    rows_ref[...] = codes & (ROWS - 1)
    copies = [pltpu.make_async_copy(rows_ref.at[u], smem[u], sem.at[u]) for u in range(LINES)]
    for c in copies:
        c.start()
    return copies


def slotted(values, slot):
    return [jnp.where(slot == s, values, 0.0) for s in range(4)]


def spaced(pieces):
    blank = jnp.zeros((16, LINE), bf16)
    return jnp.concatenate([v for p in pieces for v in (blank, p.astype(bf16))], axis=0)


def vals_rows(group, k, start, count):
    return pl.ds((group * LINE + start) * 8 + k, count, stride=8)


def place_pair(first, second, same, eye, vals_ref, group, k):
    second = [b + jnp.where(same, a, 0.0) for a, b in zip(first, second)]
    first, second = spaced(first), spaced(second)
    for h in range(2):
        at = slice(256 * h, 256 * h + 256)
        block = nt(eye, jnp.concatenate([first[:, at], second[:, at]], axis=0))
        vals_ref[vals_rows(group, k, 256 * h, 256), :] = block[:, :128]
        vals_ref[vals_rows(group, k + 4, 256 * h, 256), :] = block[:, 128:]


def looked_up(vals_ref, slot, pick, group, k):
    rows = vals_ref[vals_rows(group, k, 0, LINE), :].astype(bf16)
    parts = nt(pick, rows)
    out = parts[:16]
    for s in range(1, 4):
        out = jnp.where(slot == s, parts[s * 16 : (s + 1) * 16], out)
    return out


def walk(smem, vals_ref, tables, start, stop):
    sub = lax.broadcasted_iota(jnp.int32, (8, 128), 0)

    def one(g):
        for group in range(LINES // 8):
            here = pl.ds(pl.multiple_of((group * LINE + g) * 8, 8), 8)
            tile = vals_ref[here, :]
            at = [pl.ds(smem[group * 8 + k][g] + (8 - k), 8) for k in range(8)]
            rows = [tables[k % TABLES][at[k], :] for k in range(8)]
            for k in range(8):
                pltpu.store(tables[k % TABLES].at[at[k], :], rows[k] + tile, mask=sub == k)
            out = rows
            for bit in (1, 2, 4):
                out = [jnp.where((sub & bit) != 0, b, a) for a, b in zip(out[::2], out[1::2])]
            vals_ref[here, :] = out[0]

    def step(i, carry):
        one(start + 2 * i)
        one(start + 2 * i + 1)
        return carry

    lax.fori_loop(0, (stop - start) // 2, step, 0)


def quantize_kernel(before_ref, head_ref, tail_ref, after_ref, values_ref, weights_ref, fine_codes_ref, coarse_codes_ref,
                    eye_ref, pick_ref, pick_sum_ref, table_in, fine_error_ref, coarse_error_ref, keep_ref, send_ref,
                    t0, t1, t2, t3, vals_ref, enc_ref, fine_padded, coarse_padded, fine_rows, coarse_rows, *rest):
    fine_smem, coarse_smem, (fine_sem, coarse_sem, in_sem) = rest[:LINES], rest[LINES : 2 * LINES], rest[2 * LINES :]
    tables = [t0, t1, t2, t3]
    fetch = pltpu.make_async_copy(table_in, t0.at[pl.ds(8, ROWS), :], in_sem)
    fetch.start()
    gap = jnp.zeros((LINES, ROW - WIDTH), jnp.int32)
    fine_padded[...] = jnp.concatenate([fine_codes_ref[:, :WIDTH], gap, fine_codes_ref[:, WIDTH:], gap], axis=1)
    fine_copies = put_rows(fine_padded[...], fine_rows, fine_smem, fine_sem)
    gap = jnp.zeros((1, LINE - TILE), jnp.int32)
    for u in range(LINES):
        coarse_padded[u : u + 1, :] = jnp.concatenate([coarse_codes_ref[:, u * TILE : (u + 1) * TILE], gap], axis=1)
    coarse_copies = put_rows(coarse_padded[...], coarse_rows, coarse_smem, coarse_sem)
    weights, eye, pick, pick_sum = weights_ref[...], eye_ref[...], pick_ref[...], pick_sum_ref[...]

    def encoded(u):
        lines = [r[u].astype(f32) for r in (before_ref, head_ref, tail_ref, after_ref)]
        moved = [[pltpu.roll(v, 1, 1) for v in lines], lines, [pltpu.roll(v, ROW - 1, 1) for v in lines]]
        pieces = []
        for r in range(3):
            for m in moved:
                pieces.append(jnp.concatenate([m[r], m[r + 1]], axis=1).astype(bf16))
        stacked = jnp.concatenate(pieces, axis=0)
        enc = jnp.concatenate([lines[1], lines[2]], axis=1) + jnp.dot(weights, stacked, preferred_element_type=f32)
        enc_ref[u] = enc
        return slotted(enc, fine_padded[pl.ds(u, 1), :] >> 14)

    def encode(group, carry):
        for k in range(4):
            u = 8 * group + k
            same = fine_rows[pl.ds(u, 1), :] == fine_rows[pl.ds(u + 4, 1), :]
            place_pair(encoded(u), encoded(u + 4), same, eye, vals_ref, group, k)
        return carry

    lax.fori_loop(0, LINES // 8, encode, 0)
    fetch.wait()

    def spread(i, carry):
        at = pl.ds(pl.multiple_of(i * 64 + 8, 8), 64)
        code_part = t0[at, :]
        for t in tables[1:]:
            t[at, :] = code_part
        return carry

    lax.fori_loop(0, ROWS // 64, spread, 0)
    for c in fine_copies:
        c.wait()
    walk(fine_smem, vals_ref, tables, 0, WIDTH)
    walk(fine_smem, vals_ref, tables, ROW, ROW + WIDTH)

    tail_gap = jnp.zeros((CHANNELS, LINE - TILE), f32)

    def slots_of(u):
        values = jnp.concatenate([values_ref[u].astype(f32), tail_gap], axis=1)
        return slotted(values, coarse_padded[pl.ds(u, 1), :] >> 14)

    def turn(group, carry):
        for k in range(8):
            u = 8 * group + k
            error = enc_ref[u] - looked_up(vals_ref, fine_padded[pl.ds(u, 1), :] >> 14, pick, group, k)
            fine_error_ref[u] = jnp.concatenate([error[:, :WIDTH], error[:, ROW : ROW + WIDTH]], axis=1).astype(bf16)
        for k in range(4):
            u = 8 * group + k
            same = coarse_rows[pl.ds(u, 1), :] == coarse_rows[pl.ds(u + 4, 1), :]
            place_pair(slots_of(u), slots_of(u + 4), same, eye, vals_ref, group, k)
        return carry

    lax.fori_loop(0, LINES // 8, turn, 0)
    for c in coarse_copies:
        c.wait()
    walk(coarse_smem, vals_ref, tables, 0, TILE)
    my_x, my_y, my_z, my_core = (lax.axis_index(a) for a in ("x", Y, "z", "core"))

    def total(i, carry):
        for n, out_ref, core in ((0, send_ref, 1 - my_core), (0, keep_ref, my_core),
                                 (1, send_ref, 1 - my_core), (1, keep_ref, my_core)):
            b = 4 * i + 2 * n + core
            at = pl.ds(pl.multiple_of(b * 256 + 8, 8), 256)
            summed = t0[at, :] + t1[at, :] + t2[at, :] + t3[at, :]
            parts = nt(pick_sum, summed.astype(bf16)).astype(bf16)
            y_off = ((b >> 4) - my_y) & 3
            z_off = ((b >> 1) & 7) ^ my_z
            z_top = z_off >> 2
            z_at = z_off ^ (3 * z_top)
            for s in range(4):
                x_off = (s - my_x) & 3
                place = (jnp.where(core == 0, x_off, y_off), jnp.where(core == 0, y_off, x_off), z_at)
                out_ref[place] = parts[s * 16 : (s + 1) * 16]
        return carry

    lax.fori_loop(0, ROWS // 1024, total, 0)
    for q in range(LINES // 4):
        parts = []
        for k in range(4):
            u = 4 * q + k
            looked = looked_up(vals_ref, coarse_padded[u : u + 1, :] >> 14, pick, u // 8, u % 8)
            parts.append(values_ref[u].astype(f32) - looked[:, :TILE])
        coarse_error_ref[0, :, q * 4 * TILE : (q + 1) * 4 * TILE] = jnp.concatenate(parts, axis=1).astype(bf16)


def quantize(before, head, tail, after, values, weights, fine_codes, coarse_codes, table):
    sums = jax.ShapeDtypeStruct((4, 4, 8, CHANNELS, 256), bf16)
    return pl.pallas_call(
        quantize_kernel,
        out_shape=[jax.ShapeDtypeStruct((LINES, CHANNELS, TILE), bf16),
                   jax.ShapeDtypeStruct((1, CHANNELS, LINES * TILE), bf16), sums, sums],
        in_specs=[VMEM] * 11 + [HBM],
        out_specs=[VMEM] * 4,
        scratch_shapes=[pltpu.VMEM((ROWS + 16, 128), f32)] * TABLES
        + [pltpu.VMEM((LINES * LINE, 128), f32), pltpu.VMEM((LINES, CHANNELS, LINE), f32)]
        + [pltpu.VMEM((LINES, LINE), jnp.int32)] * 4
        + [pltpu.SMEM((LINE,), jnp.int32)] * (2 * LINES)
        + [pltpu.SemaphoreType.DMA((LINES,)), pltpu.SemaphoreType.DMA((LINES,)), pltpu.SemaphoreType.DMA],
        name="quantize",
        compiler_params=pltpu.CompilerParams(vmem_limit_bytes=50 * MIB),
        cost_estimate=pl.CostEstimate(flops=10**9, bytes_accessed=10**8, transcendentals=0),
    )(before, head, tail, after, values, weights, fine_codes, coarse_codes, identity(), pick_matrix(0), pick_matrix(16), table)


def device_of(x, y, z, core):
    return ((x % 4 * 4 + y % 4) * 8 + z) * 2 + core


def permuted(value, target):
    pairs = [(device_of(x, y, z, c), device_of(*target(x, y, z, c)))
             for x in range(4) for y in range(4) for z in range(8) for c in range(2)]
    return lax.ppermute(value, CORES, pairs)


def along(first, k):
    def target(x, y, z, c):
        return (x + k, y, z, c) if (c == 0) == first else (x, y + k, z, c)
    return target


def across(bits):
    return lambda x, y, z, c: (x, y, z ^ bits, c)


def add_kernel(n_in, *refs):
    ins, outs = refs[:n_in], refs[n_in:]
    rows = ins[0].shape[0] // len(outs)

    def piece(k, i):
        total = ins[0][k * rows + i].astype(f32)
        for r in ins[1:]:
            total = total + r[k * rows + i].astype(f32)
        outs[k][i] = total.astype(outs[k].dtype)

    for k in range(len(outs)):
        if rows <= 4:
            for i in range(rows):
                piece(k, i)
        else:
            def several(j, carry, k=k):
                for i in range(4):
                    piece(k, 4 * j + i)
                return carry
            lax.fori_loop(0, rows // 4, several, 0)


def added(ways, *parts):
    share = parts[0].shape[0] // ways
    shapes = [jax.ShapeDtypeStruct((share, CHANNELS, 256), f32 if k == 0 else bf16) for k in range(ways)]
    return pl.pallas_call(
        functools.partial(add_kernel, len(parts)),
        out_shape=shapes,
        in_specs=[VMEM] * len(parts),
        out_specs=[VMEM] * ways,
        name="add",
        compiler_params=pltpu.CompilerParams(vmem_limit_bytes=16 * MIB),
    )(*parts)


def shared_sums(keep, send):
    keep, send = (v.reshape(128, CHANNELS, 256) for v in (keep, send))
    own, *sends = added(4, keep, permuted(send, lambda x, y, z, c: (x, y, z, 1 - c)))
    for first in (True, False):
        got = [permuted(sends[k - 1], along(first, k)) for k in (2, 1, 3)]
        own, *sends = added(4 if first else 2, own, *got)
    for bits, ways in ((7, 2), (2, 2), (1, 1)):
        own, *sends = added(ways, own, permuted(sends[0], across(bits)))
    return own[0]


def shards(latents, conv_kernel, codebook, fine_codes, coarse_codes):
    head, tail, lifted = lift(latents)
    size = lax.axis_size(SPACE)
    up = [(i, i + 1) for i in range(size - 1)]
    before = lax.ppermute(tail, SPACE, up)
    after = lax.ppermute(head, SPACE, [(j, i) for i, j in up])
    table = code_table(codebook)
    moved = lax.all_to_all(lifted, SPACE, split_axis=0, concat_axis=0, tiled=True)
    fine_error, coarse_error, keep, send = quantize(
        before, head, tail, after, moved, conv_kernel, fine_codes, coarse_codes, table)
    return fine_error, coarse_error, shared_sums(keep, send)


def solution(mesh):
    split = Mesh(mesh.devices.reshape(4, 2, 2, 8, 2), CORES)
    return jax.shard_map(
        shards,
        mesh=split,
        in_specs=(P(FRAMES_BY, None, SPACE), P(), P(), P(FRAMES_BY, SPACE), P(CORES, None)),
        out_specs=(P(FRAMES_BY, None, SPACE), P(CORES, None, None), P(None, CORES)),
        check_vma=False,
    )
```
